512 devices in a mesh: rep: 16 (over y, x_hi), grp: 32 (over z, x_lo, core).
Axes of the slice: x: 4 (x_hi: 2, x_lo: 2; x = x_hi * 2 + x_lo), y: 8, z: 8, core: 2. Of those that a mesh axis runs over, the one named last changes fastest.
Arguments:
- grad_parts: bfloat16 [16, 2, 5120, 2048], P('rep', None, 'grp'), may hold values from -6 to 6
- master: float32 [2, 5120, 2048], P(None, 'grp', 'rep'), may hold values from -0.078125 to 0.078125
- first_moment: float32 [2, 5120, 2048], P(None, 'grp', 'rep'), may hold values from -2.4 to 2.4
- second_moment: float32 [2, 5120, 2048], P(None, 'grp', 'rep'), may hold values from 0.002 to 0.2
- actor_weights: bfloat16 [2, 2048, 5120], P(None, 'grp'), may hold values from -0.119628906 to 0.119628906
Outputs:
- new_actor: bfloat16 [2, 2048, 5120], P(None, 'grp')
- new_master: float32 [2, 5120, 2048], P(None, 'grp', 'rep')
- new_first: float32 [2, 5120, 2048], P(None, 'grp', 'rep')
- new_second: float32 [2, 5120, 2048], P(None, 'grp', 'rep')
The draws below stay inside these ranges and needn't reach their ends.
All inputs are finite; a program needn't handle non-finite values.
Results may differ from the reference program's by a relative error of at most 0.014.
Values may be sent and summed in bfloat16 or wider, within the bound.
A program may use at most 64 MiB of HBM per device.

```python
import math
import jax
import jax.numpy as jnp
from jax import lax

D = 5120
LAYERS = 2
KVW = 2048
N_REP = 16


def level_of(own_key, dims, shards, least, largest):
    level = 1.0
    for position, blocks in shards:
        steps = jax.random.uniform(jax.random.fold_in(jax.random.fold_in(own_key, 6), position), (blocks,), jnp.float32, least / len(shards), largest / len(shards))
        level = level * jnp.repeat(jnp.exp(steps), dims[position] // blocks).reshape((-1,) + (1,) * (len(dims) - 1 - position))
    return level


def centred(stream_key, extent, width, bound, split=(), kind=jnp.bfloat16):
    entries = width * jax.random.normal(stream_key, extent, jnp.float32)
    if split:
        entries = entries * level_of(stream_key, extent, split, -0.22, 0.18)
    return jnp.clip(entries, -bound, bound).astype(kind)


def setup_inputs(seed: int = 0) -> dict:
    seeds = jax.random.split(jax.random.key(seed), 6)
    grad_parts = centred(seeds[0], (N_REP, LAYERS, D, KVW), 1.0, 6.0, ((0, 16), (2, 32)))
    master = centred(seeds[1], (LAYERS, D, KVW), D ** -0.5, 0.078125, ((1, 32), (2, 16)), jnp.float32)
    first_moment = centred(seeds[2], (LAYERS, D, KVW), 0.4, 2.4, ((1, 32), (2, 16)), jnp.float32)
    second_moment = jnp.clip(jnp.exp(math.log(0.2) - 4.6051702 * jax.random.uniform(seeds[3], (LAYERS, D, KVW), jnp.float32) ** level_of(seeds[3], (LAYERS, D, KVW), ((1, 32), (2, 16)), -0.2, 0.2)), 0.002, 0.2)
    actor_weights = centred(seeds[4], (LAYERS, KVW, D), 0.02, 0.119628906, ((1, 32),))
    return dict(grad_parts=grad_parts, master=master, first_moment=first_moment, second_moment=second_moment, actor_weights=actor_weights)


bias_one = 0.9999734386011124
bias_two = 0.09520785288629106
learn_rate = 0.01
decay_rate = 0.1

def adam_step(grad, master, first_moment, second_moment):
    new_first = 0.9 * first_moment + 0.1 * grad
    new_second = 0.999 * second_moment + 0.001 * grad * grad
    update = new_first / bias_one / (jnp.sqrt(new_second / bias_two) + 1e-08) + decay_rate * master
    new_master = master - learn_rate * update
    delta = (-learn_rate * update).astype(jnp.bfloat16)
    return (delta, new_master, new_first, new_second)

def reference(grad_parts, master, first_moment, second_moment, actor_weights):

    def accumulate(index, total):
        return total + grad_parts[index].astype(jnp.float32)
    grad = lax.fori_loop(0, grad_parts.shape[0], accumulate, jnp.zeros(master.shape, jnp.float32))
    delta, new_master, new_first, new_second = adam_step(grad, master, first_moment, second_moment)
    moved = jnp.swapaxes(delta, 1, 2)
    new_actor = (actor_weights.astype(jnp.float32) + moved.astype(jnp.float32)).astype(jnp.bfloat16)
    return (new_actor, new_master, new_first, new_second)
```

```python
import jax
import jax.numpy as jnp
from jax import lax
from jax.experimental import pallas as pl
from jax.experimental.pallas import tpu as pltpu
from jax.sharding import PartitionSpec as P

MESH = pl.DeviceIdType.MESH

bias_one = 0.9999734386011124
bias_two = 0.09520785288629106
learn_rate = 0.01
decay_rate = 0.1

NY = 8
LAYERS = 2
ROWS = 160
HALF = ROWS // 2
COLS = 128
PIECE = 16
SPAN = 640
Z_ORDER = (0, 4, 2, 6, 1, 5, 3, 7)
F32 = jnp.float32
BF16 = jnp.bfloat16


def kernel(
    grad, master, first, second, actor,
    new_actor, new_master, new_first, new_second,
    grad_v, master_v, first_v, second_v, actor_v,
    sum_recv, sum_send, one_recv, one_send, swapped, total, cross_send, cross_recv,
    padded, delta_send, delta_recv, piece,
    load_sem, store_sem, rs_send, rs_recv, swap_sems, cross_sems, move_send, move_recv, ag_send, ag_recv, ag_cross, ag_over, piece_sem,
):
    r, g = lax.axis_index("rep"), lax.axis_index("grp")
    y, h = r // 2, r % 2
    z, lo, core = g // 4, (g // 2) % 2, g % 2
    ring = (((y + 1) % NY) * 2 + h, ((y + NY - 1) % NY) * 2 + h)
    beyond = (((y + 2) % NY) * 2 + h, ((y + NY - 2) % NY) * 2 + h)
    partner = y * 2 + (1 - h)

    def at(dy):
        return (y + dy + 2 * NY) % NY

    def flip(bit, by):
        return (bit + by) % 2

    def remote(source, target, send_sem, recv_sem, rep, grp):
        return pltpu.make_async_remote_copy(
            src_ref=source, dst_ref=target, send_sem=send_sem, recv_sem=recv_sem,
            device_id={"rep": rep, "grp": grp}, device_id_type=MESH,
        )

    grad_load = pltpu.make_async_copy(grad.at[0], grad_v, load_sem.at[0])
    grad_load.start()
    unit = pl.ds(pl.multiple_of((y // 2) * PIECE, PIECE), PIECE)
    first_z = 2 * flip(h, core) + 1 - y % 2
    loads = [
        pltpu.make_async_copy(master, master_v, load_sem.at[1]),
        pltpu.make_async_copy(first, first_v, load_sem.at[2]),
        pltpu.make_async_copy(second, second_v, load_sem.at[3]),
    ]
    for t in range(2):
        rows = pl.ds(pl.multiple_of((first_z + 4 * t) * SPAN, 128), SPAN)
        loads.append(pltpu.make_async_copy(actor.at[:, unit, rows], actor_v.at[t], load_sem.at[4 + t]))
    for load in loads:
        load.start()

    def target(to, other):
        return (2 * to + 1 - z % 2) * 2 + flip((z // 2) % 2, other), 2 * r + other

    barrier = pltpu.get_barrier_semaphore()
    greeted = [(peer, g) for peer in (*ring, *beyond, partner)]
    greeted += [target(to, other) for to in range(4) for other in range(2)]
    greeted += [(2 * z + lo, 4 * (first_z + 4 * t) + j) for t in range(2) for j in range(4)]
    for rep, grp in greeted:
        pl.semaphore_signal(barrier, inc=1, device_id={"rep": rep, "grp": grp}, device_id_type=MESH)
    padded[...] = jnp.zeros_like(padded)
    pl.semaphore_wait(barrier, len(greeted))

    def dest_of(way, hops):
        return at(hops if way == 0 else -hops)

    def both(dest):
        return pl.ds(pl.multiple_of(dest * 2 * COLS, 2 * COLS), 2 * COLS)

    def one(dest, owner):
        return pl.ds(pl.multiple_of((dest * 2 + owner) * COLS, COLS), COLS)

    def rs_copy(way, hops, layer, half, own=False):
        rows = pl.ds(half * HALF, HALF)
        if layer == 1:
            source, place = one_send.at[way, hops - 1, rows], one_recv.at[way, hops - 1, rows]
        else:
            place = sum_recv.at[way, hops - 1, rows]
            source = grad_v.at[0, rows, both(dest_of(way, hops))] if own else sum_send.at[way, hops - 1, rows]
        return remote(
            source, place, rs_send.at[way, hops - 1, layer, half], rs_recv.at[way, hops - 1, layer, half],
            beyond[way] if hops == 4 else ring[way], g,
        )

    def swap(offset):
        return remote(
            grad_v.at[1, :, one(at(offset), 1 - h)], swapped.at[offset % NY],
            swap_sems.at[0, offset % NY], swap_sems.at[1, offset % NY], partner, g,
        )

    sent = []

    def start(copy):
        copy.start()
        sent.append(copy)

    def rows_of(half):
        return pl.ds(half * HALF, HALF)

    def with_swapped(offset, rows):
        return grad_v[1, rows, one(at(offset), h)].astype(F32) + swapped[offset % NY, rows, :].astype(F32)

    grad_load.wait()
    start(swap(4))
    for half in range(2):
        start(rs_copy(half, 4, 0, half, True))
        for way in range(2):
            start(rs_copy(way, 3, 0, half, True))
    for offset in (3, -3, 2, -2, 1, -1, 0):
        start(swap(offset))
    swap(4).wait_recv()
    for way in range(2):
        one_send[way, 3, rows_of(way), :] = with_swapped(4, rows_of(way)).astype(BF16)
        start(rs_copy(way, 4, 1, way))
    for way in range(2):
        swap(3 if way == 0 else -3).wait_recv()
        for half in range(2):
            one_send[way, 2, rows_of(half), :] = with_swapped(3 if way == 0 else -3, rows_of(half)).astype(BF16)
            start(rs_copy(way, 3, 1, half))
    for hops in (2, 1):
        for half in range(2):
            for way in range(2):
                rows = rows_of(half)
                rs_copy(way, hops + 1, 0, half, True).wait_recv()
                summed = grad_v[0, rows, both(dest_of(way, hops))].astype(F32)
                summed = summed + sum_recv[way, hops, rows, :].astype(F32)
                if hops == 2 and half == way:
                    rs_copy(way, 4, 0, half, True).wait_recv()
                    summed = summed + sum_recv[way, 3, rows, :].astype(F32)
                sum_send[way, hops - 1, rows, :] = summed.astype(BF16)
                start(rs_copy(way, hops, 0, half))
        for way in range(2):
            swap(hops if way == 0 else -hops).wait_recv()
        for half in range(2):
            for way in range(2):
                rows = rows_of(half)
                rs_copy(way, hops + 1, 1, half).wait_recv()
                summed = with_swapped(hops if way == 0 else -hops, rows) + one_recv[way, hops, rows, :].astype(F32)
                if hops == 2 and half == way:
                    rs_copy(way, 4, 1, half).wait_recv()
                    summed = summed + one_recv[way, 3, rows, :].astype(F32)
                one_send[way, hops - 1, rows, :] = summed.astype(BF16)
                start(rs_copy(way, hops, 1, half))

    def cross(half):
        rows = rows_of(half)
        return remote(
            cross_send.at[rows], cross_recv.at[rows], cross_sems.at[0, half], cross_sems.at[1, half], partner, g
        )

    for half in range(2):
        for way in range(2):
            rs_copy(way, 1, 0, half).wait_recv()
        rows = rows_of(half)

        def last(owner, rows=rows):
            side = pl.ds(pl.multiple_of(owner * COLS, COLS), COLS)
            summed = grad_v[0, rows, one(y, owner)].astype(F32)
            for way in range(2):
                summed = summed + sum_recv[way, 0, rows, side].astype(F32)
            return summed

        cross_send[rows, :] = last(1 - h).astype(BF16)
        start(cross(half))
        total[0, rows, :] = last(h)
    swap(0).wait_recv()
    for half in range(2):
        for way in range(2):
            rs_copy(way, 1, 1, half).wait_recv()
        rows = rows_of(half)
        summed = with_swapped(0, rows)
        for way in range(2):
            summed = summed + one_recv[way, 0, rows, :].astype(F32)
        total[1, rows, :] = summed

    for load in loads:
        load.wait()
    slot = (z // 4) * 4 + g % 4
    shift = pl.multiple_of((g % 4) * 32, 32)
    stores = []
    for layer in (1, 0):
        gradient = total[layer]
        if layer == 0:
            for half in range(2):
                cross(half).wait_recv()
            gradient = gradient + cross_recv[...].astype(F32)
        moment = 0.9 * first_v[layer] + 0.1 * gradient
        square = 0.999 * second_v[layer] + 0.001 * gradient * gradient
        weight = master_v[layer]
        update = moment * (1.0 / bias_one) / (jnp.sqrt(square * (1.0 / bias_two)) + 1e-08) + decay_rate * weight
        step = -learn_rate * update
        padded[layer, pl.ds(shift, ROWS), :] = step
        delta_send[layer] = padded[layer].T.astype(BF16)
        for to in range(4):
            for other in range(2):
                start(
                    remote(
                        delta_send.at[layer, pl.ds(other * 64 + to * PIECE, PIECE)], delta_recv.at[layer, slot],
                        move_send.at[layer, to, other], move_recv.at[layer], *target(to, other),
                    )
                )
        master_v[layer] = weight + step
        first_v[layer] = moment
        second_v[layer] = square
        for index, (array, result) in enumerate(
            ((master_v, new_master), (first_v, new_first), (second_v, new_second))
        ):
            store = pltpu.make_async_copy(array.at[layer], result.at[layer], store_sem.at[index, layer])
            store.start()
            stores.append(store)

    def region(origin, owner, layer, half=None):
        z_block = (1 - origin % 2) * 4 + flip(owner, core) * 2
        z_range = pl.ds(z_block, 2) if half is None else pl.ds(z_block + half, 1)
        return new_actor.at[layer, z_range, pl.ds(pl.multiple_of((origin // 2) * PIECE, PIECE), PIECE)]

    def ag_copy(way, hops, layer, other):
        owner = 1 - h if other else h
        held = 2 if hops == 4 else hops - 1
        place = region(at(-held if way == 0 else held), owner, layer, way if hops == 4 else None)
        source = piece.at[layer] if hops == 1 and not other else place
        return remote(
            source, place,
            ag_send.at[way, hops - 1, layer, other], ag_recv.at[way, hops - 1, layer, other],
            beyond[way] if hops == 4 else ring[way], g,
        )

    def ag_cross_copy(layer):
        return remote(
            piece.at[layer], region(y, h, layer), ag_cross.at[0, layer], ag_cross.at[1, layer], partner, g
        )

    for layer in (1, 0):
        pltpu.make_async_copy(delta_recv.at[layer], delta_recv.at[layer], move_recv.at[layer]).wait()
        for t in range(2):
            low = [delta_recv[layer, 4 * t + j, :, :128].astype(F32) for j in range(4)]
            high = [delta_recv[layer, 4 * t + j, :, 128:].astype(F32) for j in range(4)]
            tiles = [low[0], high[0] + low[1], high[1] + low[2], high[2] + low[3], high[3]]
            for index, tile in enumerate(tiles):
                place = slice(index * 128, index * 128 + 128)
                piece[layer, t, :, place] = (actor_v[t, layer, :, place].astype(F32) + tile).astype(BF16)
        for way in range(2):
            start(ag_copy(way, 1, layer, 0))
        if layer == 0:
            start(ag_cross_copy(0))
            start(ag_cross_copy(1))
        store = pltpu.make_async_copy(piece.at[layer], region(y, h, layer), piece_sem.at[layer])
        store.start()
        stores.append(store)

    def over(hops, way, other):
        place = region(at(-hops if way == 0 else hops), 1 - h if other else h, 1, way if hops == 4 else None)
        return remote(place, place, ag_over.at[0, way, hops - 1], ag_over.at[1, way, hops - 1], partner, g)

    def gather(hops, layer, other, last=False):
        for way in range(2):
            for come in (3, 4) if last else (hops,):
                if come == 0:
                    ag_cross_copy(layer).wait_recv() if way == 0 else None
                else:
                    ag_copy(way, come, layer, other).wait_recv()
                if come == 2:
                    start(ag_copy(way, 4, layer, other))
                if come < 3:
                    start(ag_copy(way, come + 1, layer, other))
                if layer == 1:
                    start(over(come, way, 0))

    gather(1, 1, 0)
    gather(1, 0, 0)
    gather(0, 0, 1)
    gather(2, 1, 0)
    gather(2, 0, 0)
    gather(1, 0, 1)
    gather(3, 1, 0, True)
    gather(2, 0, 1)
    gather(3, 0, 0, True)
    gather(3, 0, 1, True)
    ag_cross_copy(1).wait_recv()
    for hops in (1, 2, 3, 4):
        for way in range(2):
            over(hops, way, 1).wait_recv()

    for copy in sent:
        copy.wait_send()
    for store in stores:
        store.wait()


def place_kernel(actor, master, first, second, new_actor, new_master, new_first, new_second, sems):
    copies = [
        pltpu.make_async_copy(
            actor.at[:, index], new_actor.at[:, :, pl.ds(place * SPAN, SPAN)], sems.at[index]
        )
        for index, place in enumerate(Z_ORDER)
    ]
    for index, (array, result) in enumerate(((master, new_master), (first, new_first), (second, new_second))):
        copies.append(pltpu.make_async_copy(array, result, sems.at[NY + index]))
    for copy in copies:
        copy.start()
    for copy in copies:
        copy.wait()


def body(grad_parts, master, first_moment, second_moment, actor_weights):
    args = [
        pltpu.with_memory_space_constraint(array, pltpu.HBM)
        for array in (grad_parts, master, first_moment, second_moment, actor_weights)
    ]
    anywhere = pl.BlockSpec(memory_space=pl.ANY)
    state = jax.ShapeDtypeStruct(master.shape, F32)
    state_v = pltpu.VMEM((LAYERS, ROWS, COLS), F32)
    dma = pltpu.SemaphoreType.DMA
    results = pl.pallas_call(
        kernel,
        out_shape=(jax.ShapeDtypeStruct((LAYERS, NY, 64, SPAN), BF16), state, state, state),
        in_specs=[anywhere] * 5,
        out_specs=[anywhere] * 4,
        scratch_shapes=[
            pltpu.VMEM((LAYERS, ROWS, 2048), BF16),
            state_v,
            state_v,
            state_v,
            pltpu.VMEM((2, LAYERS, PIECE, SPAN), BF16),
            pltpu.VMEM((2, 4, ROWS, 2 * COLS), BF16),
            pltpu.VMEM((2, 2, ROWS, 2 * COLS), BF16),
            pltpu.VMEM((2, 4, ROWS, COLS), BF16),
            pltpu.VMEM((2, 4, ROWS, COLS), BF16),
            pltpu.VMEM((NY, ROWS, COLS), BF16),
            state_v,
            pltpu.VMEM((ROWS, COLS), BF16),
            pltpu.VMEM((ROWS, COLS), BF16),
            pltpu.VMEM((LAYERS, 256, COLS), F32),
            pltpu.VMEM((LAYERS, COLS, 256), BF16),
            pltpu.VMEM((LAYERS, 8, PIECE, 256), BF16),
            pltpu.VMEM((LAYERS, 2, PIECE, SPAN), BF16),
            dma((6,)),
            dma((3, LAYERS)),
            dma((2, 4, LAYERS, 2)),
            dma((2, 4, LAYERS, 2)),
            dma((2, NY)),
            dma((2, 2)),
            dma((LAYERS, 4, 2)),
            dma((LAYERS,)),
            dma((2, 4, LAYERS, 2)),
            dma((2, 4, LAYERS, 2)),
            dma((2, LAYERS)),
            dma((2, 2, 4)),
            dma((LAYERS,)),
        ],
        compiler_params=pltpu.CompilerParams(
            collective_id=0, has_side_effects=True, vmem_limit_bytes=48 * 1024 * 1024
        ),
    )(*args)
    return pl.pallas_call(
        place_kernel,
        out_shape=(jax.ShapeDtypeStruct(actor_weights.shape, BF16), state, state, state),
        in_specs=[anywhere] * 4,
        out_specs=[anywhere] * 4,
        scratch_shapes=[dma((NY + 3,))],
        compiler_params=pltpu.CompilerParams(vmem_limit_bytes=4 * 1024 * 1024),
    )(*results)


def solution(mesh):
    in_specs = (
        P("rep", None, "grp", None),
        P(None, "grp", "rep"),
        P(None, "grp", "rep"),
        P(None, "grp", "rep"),
        P(None, "grp", None),
    )
    out_specs = (
        P(None, "grp", None),
        P(None, "grp", "rep"),
        P(None, "grp", "rep"),
        P(None, "grp", "rep"),
    )
    return jax.shard_map(body, mesh=mesh, in_specs=in_specs, out_specs=out_specs, check_vma=False)
```

```python
import jax
import jax.numpy as jnp
from jax import lax
from jax.experimental import pallas as pl
from jax.experimental.pallas import tpu as pltpu
from jax.sharding import PartitionSpec as P

MESH = pl.DeviceIdType.MESH

bias_one = 0.9999734386011124
bias_two = 0.09520785288629106
learn_rate = 0.01
decay_rate = 0.1

NY = 8
LAYERS = 2
ROWS = 160
HALF = ROWS // 2
COLS = 128
PIECE = 16
SPAN = 640
Z_ORDER = (0, 4, 2, 6, 1, 5, 3, 7)
F32 = jnp.float32
BF16 = jnp.bfloat16


def kernel(
    grad, master, first, second, actor,
    new_actor, new_master, new_first, new_second,
    grad_v, master_v, first_v, second_v, actor_v,
    sum_recv, sum_send, last_recv, raw_recv, one_recv, one_send, swapped, total,
    padded, delta_send, delta_recv, piece,
    load_sem, store_sem, rs_send, rs_recv, last_sems, raw_sems, swap_sems, move_send, move_recv, ag_send, ag_recv, ag_cross, ag_over, piece_sem,
):
    r, g = lax.axis_index("rep"), lax.axis_index("grp")
    y, h = r // 2, r % 2
    z, lo, core = g // 4, (g // 2) % 2, g % 2
    ring = (((y + 1) % NY) * 2 + h, ((y + NY - 1) % NY) * 2 + h)
    beyond = (((y + 2) % NY) * 2 + h, ((y + NY - 2) % NY) * 2 + h)
    across = (((y + 1) % NY) * 2 + 1 - h, ((y + NY - 1) % NY) * 2 + 1 - h)
    partner = y * 2 + (1 - h)

    def at(dy):
        return (y + dy + 2 * NY) % NY

    def flip(bit, by):
        return (bit + by) % 2

    def remote(source, target, send_sem, recv_sem, rep, grp):
        return pltpu.make_async_remote_copy(
            src_ref=source, dst_ref=target, send_sem=send_sem, recv_sem=recv_sem,
            device_id={"rep": rep, "grp": grp}, device_id_type=MESH,
        )

    grad_load = pltpu.make_async_copy(grad.at[0], grad_v, load_sem.at[0])
    grad_load.start()
    unit = pl.ds(pl.multiple_of((y // 2) * PIECE, PIECE), PIECE)
    first_z = 2 * flip(h, core) + 1 - y % 2
    loads = [
        pltpu.make_async_copy(master, master_v, load_sem.at[1]),
        pltpu.make_async_copy(first, first_v, load_sem.at[2]),
        pltpu.make_async_copy(second, second_v, load_sem.at[3]),
    ]
    for t in range(2):
        rows = pl.ds(pl.multiple_of((first_z + 4 * t) * SPAN, 128), SPAN)
        loads.append(pltpu.make_async_copy(actor.at[:, unit, rows], actor_v.at[t], load_sem.at[4 + t]))
    for load in loads:
        load.start()

    def target(to, other):
        return (2 * to + 1 - z % 2) * 2 + flip((z // 2) % 2, other), 2 * r + other

    barrier = pltpu.get_barrier_semaphore()
    greeted = [(peer, g) for peer in (*ring, *beyond, *across, partner)]
    greeted += [target(to, other) for to in range(4) for other in range(2)]
    greeted += [(2 * z + lo, 4 * (first_z + 4 * t) + j) for t in range(2) for j in range(4)]
    for rep, grp in greeted:
        pl.semaphore_signal(barrier, inc=1, device_id={"rep": rep, "grp": grp}, device_id_type=MESH)
    padded[...] = jnp.zeros_like(padded)
    pl.semaphore_wait(barrier, len(greeted))

    def dest_of(way, hops):
        return at(hops if way == 0 else -hops)

    def both(dest):
        return pl.ds(pl.multiple_of(dest * 2 * COLS, 2 * COLS), 2 * COLS)

    def one(dest, owner):
        return pl.ds(pl.multiple_of((dest * 2 + owner) * COLS, COLS), COLS)

    def rs_copy(way, hops, layer, half, own=False):
        rows = pl.ds(half * HALF, HALF)
        if layer == 1:
            source, place = one_send.at[way, hops - 1, rows], one_recv.at[way, hops - 1, rows]
        else:
            place = sum_recv.at[way, hops - 1, rows]
            source = grad_v.at[0, rows, both(dest_of(way, hops))] if own else sum_send.at[way, hops - 1, rows]
        return remote(
            source, place, rs_send.at[way, hops - 1, layer, half], rs_recv.at[way, hops - 1, layer, half],
            beyond[way] if hops == 4 else ring[way], g,
        )

    def last_copy(way, half, other):
        rows, owner = rows_of(half), 1 - h if other else h
        return remote(
            sum_send.at[way, 0, rows, pl.ds(pl.multiple_of(owner * COLS, COLS), COLS)],
            last_recv.at[way, other, rows], last_sems.at[0, way, half, other], last_sems.at[1, way, half, other],
            across[way] if other else ring[way], g,
        )

    def raw_copy():
        return remote(
            grad_v.at[0, :, one(y, 1 - h)], raw_recv, raw_sems.at[0], raw_sems.at[1], partner, g
        )

    def swap(offset):
        return remote(
            grad_v.at[1, :, one(at(offset), 1 - h)], swapped.at[offset % NY],
            swap_sems.at[0, offset % NY], swap_sems.at[1, offset % NY], partner, g,
        )

    sent = []

    def start(copy):
        copy.start()
        sent.append(copy)

    def rows_of(half):
        return pl.ds(half * HALF, HALF)

    def with_swapped(offset, rows):
        return grad_v[1, rows, one(at(offset), h)].astype(F32) + swapped[offset % NY, rows, :].astype(F32)

    grad_load.wait()
    start(swap(4))
    for half in range(2):
        start(rs_copy(half, 4, 0, half, True))
        for way in range(2):
            start(rs_copy(way, 3, 0, half, True))
    for offset in (3, -3, 2, -2, 1, -1, 0):
        start(swap(offset))
    start(raw_copy())
    swap(4).wait_recv()
    for way in range(2):
        one_send[way, 3, rows_of(way), :] = with_swapped(4, rows_of(way)).astype(BF16)
        start(rs_copy(way, 4, 1, way))
    for way in range(2):
        swap(3 if way == 0 else -3).wait_recv()
        for half in range(2):
            one_send[way, 2, rows_of(half), :] = with_swapped(3 if way == 0 else -3, rows_of(half)).astype(BF16)
            start(rs_copy(way, 3, 1, half))
    for hops in (2, 1):
        for half in range(2):
            for way in range(2):
                rows = rows_of(half)
                rs_copy(way, hops + 1, 0, half, True).wait_recv()
                summed = grad_v[0, rows, both(dest_of(way, hops))].astype(F32)
                summed = summed + sum_recv[way, hops, rows, :].astype(F32)
                if hops == 2 and half == way:
                    rs_copy(way, 4, 0, half, True).wait_recv()
                    summed = summed + sum_recv[way, 3, rows, :].astype(F32)
                sum_send[way, hops - 1, rows, :] = summed.astype(BF16)
                if hops == 2:
                    start(rs_copy(way, 2, 0, half))
                else:
                    for other in (1, 0):
                        start(last_copy(way, half, other))
        for way in range(2):
            swap(hops if way == 0 else -hops).wait_recv()
        for half in range(2):
            for way in range(2):
                rows = rows_of(half)
                rs_copy(way, hops + 1, 1, half).wait_recv()
                summed = with_swapped(hops if way == 0 else -hops, rows) + one_recv[way, hops, rows, :].astype(F32)
                if hops == 2 and half == way:
                    rs_copy(way, 4, 1, half).wait_recv()
                    summed = summed + one_recv[way, 3, rows, :].astype(F32)
                one_send[way, hops - 1, rows, :] = summed.astype(BF16)
                start(rs_copy(way, hops, 1, half))

    raw_copy().wait_recv()
    for half in range(2):
        rows = rows_of(half)
        summed = grad_v[0, rows, one(y, h)].astype(F32) + raw_recv[rows, :].astype(F32)
        for way in range(2):
            for other in range(2):
                last_copy(way, half, other).wait_recv()
                summed = summed + last_recv[way, other, rows, :].astype(F32)
        total[0, rows, :] = summed

    def finish_one():
        swap(0).wait_recv()
        for half in range(2):
            for way in range(2):
                rs_copy(way, 1, 1, half).wait_recv()
            rows = rows_of(half)
            summed = with_swapped(0, rows)
            for way in range(2):
                summed = summed + one_recv[way, 0, rows, :].astype(F32)
            total[1, rows, :] = summed

    for load in loads:
        load.wait()
    slot = (z // 4) * 4 + g % 4
    shift = pl.multiple_of((g % 4) * 32, 32)
    stores = []
    for layer in range(LAYERS):
        if layer == 1:
            finish_one()
        gradient = total[layer]
        moment = 0.9 * first_v[layer] + 0.1 * gradient
        square = 0.999 * second_v[layer] + 0.001 * gradient * gradient
        weight = master_v[layer]
        update = moment * (1.0 / bias_one) / (jnp.sqrt(square * (1.0 / bias_two)) + 1e-08) + decay_rate * weight
        step = -learn_rate * update
        padded[layer, pl.ds(shift, ROWS), :] = step
        delta_send[layer] = padded[layer].T.astype(BF16)
        for to in range(4):
            for other in range(2):
                start(
                    remote(
                        delta_send.at[layer, pl.ds(other * 64 + to * PIECE, PIECE)], delta_recv.at[layer, slot],
                        move_send.at[layer, to, other], move_recv.at[layer], *target(to, other),
                    )
                )
        master_v[layer] = weight + step
        first_v[layer] = moment
        second_v[layer] = square
        for index, (array, result) in enumerate(
            ((master_v, new_master), (first_v, new_first), (second_v, new_second))
        ):
            store = pltpu.make_async_copy(array.at[layer], result.at[layer], store_sem.at[index, layer])
            store.start()
            stores.append(store)

    def region(origin, owner, layer, half=None):
        z_block = (1 - origin % 2) * 4 + flip(owner, core) * 2
        z_range = pl.ds(z_block, 2) if half is None else pl.ds(z_block + half, 1)
        return new_actor.at[layer, z_range, pl.ds(pl.multiple_of((origin // 2) * PIECE, PIECE), PIECE)]

    def ag_copy(way, hops, layer, other):
        owner = 1 - h if other else h
        held = 2 if hops == 4 else hops - 1
        place = region(at(-held if way == 0 else held), owner, layer, way if hops == 4 else None)
        if hops == 1:
            place = region(y, h, layer)
        return remote(
            piece.at[layer] if hops == 1 else place, place,
            ag_send.at[way, hops - 1, layer, other], ag_recv.at[way, hops - 1, layer, other],
            beyond[way] if hops == 4 else across[way] if hops == 1 and other else ring[way], g,
        )

    def ag_cross_copy(layer):
        return remote(
            piece.at[layer], region(y, h, layer), ag_cross.at[0, layer], ag_cross.at[1, layer], partner, g
        )

    for layer in range(LAYERS):
        pltpu.make_async_copy(delta_recv.at[layer], delta_recv.at[layer], move_recv.at[layer]).wait()
        for t in range(2):
            low = [delta_recv[layer, 4 * t + j, :, :128].astype(F32) for j in range(4)]
            high = [delta_recv[layer, 4 * t + j, :, 128:].astype(F32) for j in range(4)]
            tiles = [low[0], high[0] + low[1], high[1] + low[2], high[2] + low[3], high[3]]
            for index, tile in enumerate(tiles):
                place = slice(index * 128, index * 128 + 128)
                piece[layer, t, :, place] = (actor_v[t, layer, :, place].astype(F32) + tile).astype(BF16)
        for way in range(2):
            start(ag_copy(way, 1, layer, 0))
            if layer == 0:
                start(ag_copy(way, 1, 0, 1))
        start(ag_cross_copy(layer))
        store = pltpu.make_async_copy(piece.at[layer], region(y, h, layer), piece_sem.at[layer])
        store.start()
        stores.append(store)

    def over(hops, way, other):
        place = region(at(-hops if way == 0 else hops), 1 - h if other else h, 1, way if hops == 4 else None)
        return remote(place, place, ag_over.at[0, way, hops - 1], ag_over.at[1, way, hops - 1], partner, g)

    def gather(hops, layer, other, last=False):
        for way in range(2):
            for come in (3, 4) if last else (hops,):
                ag_copy(way, come, layer, other).wait_recv()
                if come == 2:
                    start(ag_copy(way, 4, layer, other))
                if come < 3:
                    start(ag_copy(way, come + 1, layer, other))
                if layer == 1:
                    start(over(come, way, 0))

    gather(1, 0, 0)
    gather(1, 1, 0)
    gather(1, 0, 1)
    gather(2, 1, 0)
    gather(2, 0, 0)
    gather(2, 0, 1)
    gather(3, 1, 0, True)
    gather(3, 0, 0, True)
    gather(3, 0, 1, True)
    for layer in range(LAYERS):
        ag_cross_copy(layer).wait_recv()
    for hops in (1, 2, 3, 4):
        for way in range(2):
            over(hops, way, 1).wait_recv()

    for copy in sent:
        copy.wait_send()
    for store in stores:
        store.wait()


def place_kernel(actor, master, first, second, new_actor, new_master, new_first, new_second, sems):
    copies = [
        pltpu.make_async_copy(
            actor.at[:, index], new_actor.at[:, :, pl.ds(place * SPAN, SPAN)], sems.at[index]
        )
        for index, place in enumerate(Z_ORDER)
    ]
    for index, (array, result) in enumerate(((master, new_master), (first, new_first), (second, new_second))):
        copies.append(pltpu.make_async_copy(array, result, sems.at[NY + index]))
    for copy in copies:
        copy.start()
    for copy in copies:
        copy.wait()


def body(grad_parts, master, first_moment, second_moment, actor_weights):
    args = [
        pltpu.with_memory_space_constraint(array, pltpu.HBM)
        for array in (grad_parts, master, first_moment, second_moment, actor_weights)
    ]
    anywhere = pl.BlockSpec(memory_space=pl.ANY)
    state = jax.ShapeDtypeStruct(master.shape, F32)
    state_v = pltpu.VMEM((LAYERS, ROWS, COLS), F32)
    dma = pltpu.SemaphoreType.DMA
    results = pl.pallas_call(
        kernel,
        out_shape=(jax.ShapeDtypeStruct((LAYERS, NY, 64, SPAN), BF16), state, state, state),
        in_specs=[anywhere] * 5,
        out_specs=[anywhere] * 4,
        scratch_shapes=[
            pltpu.VMEM((LAYERS, ROWS, 2048), BF16),
            state_v,
            state_v,
            state_v,
            pltpu.VMEM((2, LAYERS, PIECE, SPAN), BF16),
            pltpu.VMEM((2, 4, ROWS, 2 * COLS), BF16),
            pltpu.VMEM((2, 2, ROWS, 2 * COLS), BF16),
            pltpu.VMEM((2, 2, ROWS, COLS), BF16),
            pltpu.VMEM((ROWS, COLS), BF16),
            pltpu.VMEM((2, 4, ROWS, COLS), BF16),
            pltpu.VMEM((2, 4, ROWS, COLS), BF16),
            pltpu.VMEM((NY, ROWS, COLS), BF16),
            state_v,
            pltpu.VMEM((LAYERS, 256, COLS), F32),
            pltpu.VMEM((LAYERS, COLS, 256), BF16),
            pltpu.VMEM((LAYERS, 8, PIECE, 256), BF16),
            pltpu.VMEM((LAYERS, 2, PIECE, SPAN), BF16),
            dma((6,)),
            dma((3, LAYERS)),
            dma((2, 4, LAYERS, 2)),
            dma((2, 4, LAYERS, 2)),
            dma((2, 2, 2, 2)),
            dma((2,)),
            dma((2, NY)),
            dma((LAYERS, 4, 2)),
            dma((LAYERS,)),
            dma((2, 4, LAYERS, 2)),
            dma((2, 4, LAYERS, 2)),
            dma((2, LAYERS)),
            dma((2, 2, 4)),
            dma((LAYERS,)),
        ],
        compiler_params=pltpu.CompilerParams(
            collective_id=0, has_side_effects=True, vmem_limit_bytes=48 * 1024 * 1024
        ),
    )(*args)
    return pl.pallas_call(
        place_kernel,
        out_shape=(jax.ShapeDtypeStruct(actor_weights.shape, BF16), state, state, state),
        in_specs=[anywhere] * 4,
        out_specs=[anywhere] * 4,
        scratch_shapes=[dma((NY + 3,))],
        compiler_params=pltpu.CompilerParams(vmem_limit_bytes=4 * 1024 * 1024),
    )(*results)


def solution(mesh):
    in_specs = (
        P("rep", None, "grp", None),
        P(None, "grp", "rep"),
        P(None, "grp", "rep"),
        P(None, "grp", "rep"),
        P(None, "grp", None),
    )
    out_specs = (
        P(None, "grp", None),
        P(None, "grp", "rep"),
        P(None, "grp", "rep"),
        P(None, "grp", "rep"),
    )
    return jax.shard_map(body, mesh=mesh, in_specs=in_specs, out_specs=out_specs, check_vma=False)
```

```python
import jax
import jax.numpy as jnp
from jax import lax
from jax.experimental import pallas as pl
from jax.experimental.pallas import tpu as pltpu
from jax.sharding import PartitionSpec as P

MESH = pl.DeviceIdType.MESH

bias_one = 0.9999734386011124
bias_two = 0.09520785288629106
learn_rate = 0.01
decay_rate = 0.1

NY = 8
LAYERS = 2
ROWS = 160
HALF = ROWS // 2
COLS = 128
PIECE = 16
SPAN = 640
Z_ORDER = (0, 4, 2, 6, 1, 5, 3, 7)
F32 = jnp.float32
BF16 = jnp.bfloat16


def kernel(
    grad, master, first, second, actor,
    new_actor, new_master, new_first, new_second,
    grad_v, master_v, first_v, second_v, actor_v,
    sum_recv, sum_send, last_recv, raw_recv, one_recv, one_send, swapped, total,
    padded, delta_send, delta_recv, piece,
    load_sem, store_sem, rs_send, rs_recv, last_sems, raw_sems, swap_sems, move_send, move_recv, ag_send, ag_recv, ag_cross, ag_over, piece_sem,
):
    r, g = lax.axis_index("rep"), lax.axis_index("grp")
    y, h = r // 2, r % 2
    z, lo, core = g // 4, (g // 2) % 2, g % 2
    ring = (((y + 1) % NY) * 2 + h, ((y + NY - 1) % NY) * 2 + h)
    beyond = (((y + 2) % NY) * 2 + h, ((y + NY - 2) % NY) * 2 + h)
    across = (((y + 1) % NY) * 2 + 1 - h, ((y + NY - 1) % NY) * 2 + 1 - h)
    far = (((y + 2) % NY) * 2 + 1 - h, ((y + NY - 2) % NY) * 2 + 1 - h)
    partner = y * 2 + (1 - h)

    def at(dy):
        return (y + dy + 2 * NY) % NY

    def flip(bit, by):
        return (bit + by) % 2

    def remote(source, target, send_sem, recv_sem, rep, grp):
        return pltpu.make_async_remote_copy(
            src_ref=source, dst_ref=target, send_sem=send_sem, recv_sem=recv_sem,
            device_id={"rep": rep, "grp": grp}, device_id_type=MESH,
        )

    grad_load = pltpu.make_async_copy(grad.at[0], grad_v, load_sem.at[0])
    grad_load.start()
    unit = pl.ds(pl.multiple_of((y // 2) * PIECE, PIECE), PIECE)
    first_z = 2 * flip(h, core) + 1 - y % 2
    loads = [
        pltpu.make_async_copy(master, master_v, load_sem.at[1]),
        pltpu.make_async_copy(first, first_v, load_sem.at[2]),
        pltpu.make_async_copy(second, second_v, load_sem.at[3]),
    ]
    for t in range(2):
        rows = pl.ds(pl.multiple_of((first_z + 4 * t) * SPAN, 128), SPAN)
        loads.append(pltpu.make_async_copy(actor.at[:, unit, rows], actor_v.at[t], load_sem.at[4 + t]))
    for load in loads:
        load.start()

    def target(to, other):
        return (2 * to + 1 - z % 2) * 2 + flip((z // 2) % 2, other), 2 * r + other

    barrier = pltpu.get_barrier_semaphore()
    greeted = [(peer, g) for peer in (*ring, *beyond, *across, *far, partner)]
    greeted += [target(to, other) for to in range(4) for other in range(2)]
    greeted += [(2 * z + lo, 4 * (first_z + 4 * t) + j) for t in range(2) for j in range(4)]
    for rep, grp in greeted:
        pl.semaphore_signal(barrier, inc=1, device_id={"rep": rep, "grp": grp}, device_id_type=MESH)
    padded[...] = jnp.zeros_like(padded)
    pl.semaphore_wait(barrier, len(greeted))

    def dest_of(way, hops):
        return at(hops if way == 0 else -hops)

    def both(dest):
        return pl.ds(pl.multiple_of(dest * 2 * COLS, 2 * COLS), 2 * COLS)

    def one(dest, owner):
        return pl.ds(pl.multiple_of((dest * 2 + owner) * COLS, COLS), COLS)

    def rs_copy(way, hops, layer, half, own=False):
        rows = pl.ds(half * HALF, HALF)
        if layer == 1:
            source, place = one_send.at[way, hops - 1, rows], one_recv.at[way, hops - 1, rows]
        else:
            place = sum_recv.at[way, hops - 1, rows]
            source = grad_v.at[0, rows, both(dest_of(way, hops))] if own else sum_send.at[way, hops - 1, rows]
        return remote(
            source, place, rs_send.at[way, hops - 1, layer, half], rs_recv.at[way, hops - 1, layer, half],
            beyond[way] if hops == 4 else ring[way], g,
        )

    def last_copy(way, half, other):
        rows, owner = rows_of(half), 1 - h if other else h
        return remote(
            sum_send.at[way, 0, rows, pl.ds(pl.multiple_of(owner * COLS, COLS), COLS)],
            last_recv.at[way, other, rows], last_sems.at[0, way, half, other], last_sems.at[1, way, half, other],
            across[way] if other else ring[way], g,
        )

    def raw_copy():
        return remote(
            grad_v.at[0, :, one(y, 1 - h)], raw_recv, raw_sems.at[0], raw_sems.at[1], partner, g
        )

    def swap(offset):
        return remote(
            grad_v.at[1, :, one(at(offset), 1 - h)], swapped.at[offset % NY],
            swap_sems.at[0, offset % NY], swap_sems.at[1, offset % NY], partner, g,
        )

    sent = []

    def start(copy):
        copy.start()
        sent.append(copy)

    def rows_of(half):
        return pl.ds(half * HALF, HALF)

    def with_swapped(offset, rows):
        return grad_v[1, rows, one(at(offset), h)].astype(F32) + swapped[offset % NY, rows, :].astype(F32)

    grad_load.wait()
    start(swap(4))
    for half in range(2):
        start(rs_copy(half, 4, 0, half, True))
        for way in range(2):
            start(rs_copy(way, 3, 0, half, True))
    for offset in (3, -3, 2, -2, 1, -1, 0):
        start(swap(offset))
    start(raw_copy())
    swap(4).wait_recv()
    for way in range(2):
        one_send[way, 3, rows_of(way), :] = with_swapped(4, rows_of(way)).astype(BF16)
        start(rs_copy(way, 4, 1, way))
    for way in range(2):
        swap(3 if way == 0 else -3).wait_recv()
        for half in range(2):
            one_send[way, 2, rows_of(half), :] = with_swapped(3 if way == 0 else -3, rows_of(half)).astype(BF16)
            start(rs_copy(way, 3, 1, half))
    for hops in (2, 1):
        for half in range(2):
            for way in range(2):
                rows = rows_of(half)
                rs_copy(way, hops + 1, 0, half, True).wait_recv()
                summed = grad_v[0, rows, both(dest_of(way, hops))].astype(F32)
                summed = summed + sum_recv[way, hops, rows, :].astype(F32)
                if hops == 2 and half == way:
                    rs_copy(way, 4, 0, half, True).wait_recv()
                    summed = summed + sum_recv[way, 3, rows, :].astype(F32)
                sum_send[way, hops - 1, rows, :] = summed.astype(BF16)
                if hops == 2:
                    start(rs_copy(way, 2, 0, half))
                else:
                    for other in (1, 0):
                        start(last_copy(way, half, other))
        for way in range(2):
            swap(hops if way == 0 else -hops).wait_recv()
        for half in range(2):
            for way in range(2):
                rows = rows_of(half)
                rs_copy(way, hops + 1, 1, half).wait_recv()
                summed = with_swapped(hops if way == 0 else -hops, rows) + one_recv[way, hops, rows, :].astype(F32)
                if hops == 2 and half == way:
                    rs_copy(way, 4, 1, half).wait_recv()
                    summed = summed + one_recv[way, 3, rows, :].astype(F32)
                one_send[way, hops - 1, rows, :] = summed.astype(BF16)
                start(rs_copy(way, hops, 1, half))

    raw_copy().wait_recv()
    for half in range(2):
        rows = rows_of(half)
        summed = grad_v[0, rows, one(y, h)].astype(F32) + raw_recv[rows, :].astype(F32)
        for way in range(2):
            for other in range(2):
                last_copy(way, half, other).wait_recv()
                summed = summed + last_recv[way, other, rows, :].astype(F32)
        total[0, rows, :] = summed

    def finish_one():
        swap(0).wait_recv()
        for half in range(2):
            for way in range(2):
                rs_copy(way, 1, 1, half).wait_recv()
            rows = rows_of(half)
            summed = with_swapped(0, rows)
            for way in range(2):
                summed = summed + one_recv[way, 0, rows, :].astype(F32)
            total[1, rows, :] = summed

    for load in loads:
        load.wait()
    slot = (z // 4) * 4 + g % 4
    shift = pl.multiple_of((g % 4) * 32, 32)
    stores = []
    for layer in range(LAYERS):
        if layer == 1:
            finish_one()
        gradient = total[layer]
        moment = 0.9 * first_v[layer] + 0.1 * gradient
        square = 0.999 * second_v[layer] + 0.001 * gradient * gradient
        weight = master_v[layer]
        update = moment * (1.0 / bias_one) / (jnp.sqrt(square * (1.0 / bias_two)) + 1e-08) + decay_rate * weight
        step = -learn_rate * update
        padded[layer, pl.ds(shift, ROWS), :] = step
        delta_send[layer] = padded[layer].T.astype(BF16)
        for to in range(4):
            for other in range(2):
                start(
                    remote(
                        delta_send.at[layer, pl.ds(other * 64 + to * PIECE, PIECE)], delta_recv.at[layer, slot],
                        move_send.at[layer, to, other], move_recv.at[layer], *target(to, other),
                    )
                )
        master_v[layer] = weight + step
        first_v[layer] = moment
        second_v[layer] = square
        for index, (array, result) in enumerate(
            ((master_v, new_master), (first_v, new_first), (second_v, new_second))
        ):
            store = pltpu.make_async_copy(array.at[layer], result.at[layer], store_sem.at[index, layer])
            store.start()
            stores.append(store)

    def region(origin, owner, layer, half=None):
        z_block = (1 - origin % 2) * 4 + flip(owner, core) * 2
        z_range = pl.ds(z_block, 2) if half is None else pl.ds(z_block + half, 1)
        return new_actor.at[layer, z_range, pl.ds(pl.multiple_of((origin // 2) * PIECE, PIECE), PIECE)]

    def ag_copy(way, hops, layer, other):
        held = 2 if hops == 4 else hops - 1
        goes_across = other and hops in ((1,), (3, 4))[layer]
        owner = 1 - h if other and not goes_across else h
        place = region(at(-held if way == 0 else held), owner, layer, way if hops == 4 else None)
        near = across if goes_across else ring
        return remote(
            piece.at[layer] if hops == 1 else place, place,
            ag_send.at[way, hops - 1, layer, other], ag_recv.at[way, hops - 1, layer, other],
            (far if goes_across else beyond)[way] if hops == 4 else near[way], g,
        )

    def ag_cross_copy(layer):
        return remote(
            piece.at[layer], region(y, h, layer), ag_cross.at[0, layer], ag_cross.at[1, layer], partner, g
        )

    for layer in range(LAYERS):
        pltpu.make_async_copy(delta_recv.at[layer], delta_recv.at[layer], move_recv.at[layer]).wait()
        for t in range(2):
            low = [delta_recv[layer, 4 * t + j, :, :128].astype(F32) for j in range(4)]
            high = [delta_recv[layer, 4 * t + j, :, 128:].astype(F32) for j in range(4)]
            tiles = [low[0], high[0] + low[1], high[1] + low[2], high[2] + low[3], high[3]]
            for index, tile in enumerate(tiles):
                place = slice(index * 128, index * 128 + 128)
                piece[layer, t, :, place] = (actor_v[t, layer, :, place].astype(F32) + tile).astype(BF16)
        for way in range(2):
            start(ag_copy(way, 1, layer, 0))
            if layer == 0:
                start(ag_copy(way, 1, 0, 1))
        start(ag_cross_copy(layer))
        store = pltpu.make_async_copy(piece.at[layer], region(y, h, layer), piece_sem.at[layer])
        store.start()
        stores.append(store)

    def over(hops, way, other):
        place = region(at(-hops if way == 0 else hops), 1 - h if other else h, 1)
        return remote(place, place, ag_over.at[0, way, hops - 1], ag_over.at[1, way, hops - 1], partner, g)

    def gather(come, layer, other):
        for way in range(2):
            ag_copy(way, come, layer, other).wait_recv()
            for to in (4, 3) if come == 2 else (2,):
                start(ag_copy(way, to, layer, other))
                if layer == 1 and come == 2:
                    start(ag_copy(way, to, 1, 1))
            if layer == 1:
                start(over(come, way, 0))

    gather(1, 0, 0)
    gather(1, 1, 0)
    gather(1, 0, 1)
    gather(2, 1, 0)
    gather(2, 0, 0)
    gather(2, 0, 1)
    for layer in range(LAYERS):
        ag_cross_copy(layer).wait_recv()
    for way in range(2):
        for hops in (1, 2):
            over(hops, way, 1).wait_recv()
        for hops in (3, 4):
            for layer in range(LAYERS):
                for other in range(2):
                    ag_copy(way, hops, layer, other).wait_recv()

    for copy in sent:
        copy.wait_send()
    for store in stores:
        store.wait()


def place_kernel(actor, master, first, second, new_actor, new_master, new_first, new_second, sems):
    copies = [
        pltpu.make_async_copy(
            actor.at[:, index], new_actor.at[:, :, pl.ds(place * SPAN, SPAN)], sems.at[index]
        )
        for index, place in enumerate(Z_ORDER)
    ]
    for index, (array, result) in enumerate(((master, new_master), (first, new_first), (second, new_second))):
        copies.append(pltpu.make_async_copy(array, result, sems.at[NY + index]))
    for copy in copies:
        copy.start()
    for copy in copies:
        copy.wait()


def body(grad_parts, master, first_moment, second_moment, actor_weights):
    args = [
        pltpu.with_memory_space_constraint(array, pltpu.HBM)
        for array in (grad_parts, master, first_moment, second_moment, actor_weights)
    ]
    anywhere = pl.BlockSpec(memory_space=pl.ANY)
    state = jax.ShapeDtypeStruct(master.shape, F32)
    state_v = pltpu.VMEM((LAYERS, ROWS, COLS), F32)
    dma = pltpu.SemaphoreType.DMA
    results = pl.pallas_call(
        kernel,
        out_shape=(jax.ShapeDtypeStruct((LAYERS, NY, 64, SPAN), BF16), state, state, state),
        in_specs=[anywhere] * 5,
        out_specs=[anywhere] * 4,
        scratch_shapes=[
            pltpu.VMEM((LAYERS, ROWS, 2048), BF16),
            state_v,
            state_v,
            state_v,
            pltpu.VMEM((2, LAYERS, PIECE, SPAN), BF16),
            pltpu.VMEM((2, 4, ROWS, 2 * COLS), BF16),
            pltpu.VMEM((2, 2, ROWS, 2 * COLS), BF16),
            pltpu.VMEM((2, 2, ROWS, COLS), BF16),
            pltpu.VMEM((ROWS, COLS), BF16),
            pltpu.VMEM((2, 4, ROWS, COLS), BF16),
            pltpu.VMEM((2, 4, ROWS, COLS), BF16),
            pltpu.VMEM((NY, ROWS, COLS), BF16),
            state_v,
            pltpu.VMEM((LAYERS, 256, COLS), F32),
            pltpu.VMEM((LAYERS, COLS, 256), BF16),
            pltpu.VMEM((LAYERS, 8, PIECE, 256), BF16),
            pltpu.VMEM((LAYERS, 2, PIECE, SPAN), BF16),
            dma((6,)),
            dma((3, LAYERS)),
            dma((2, 4, LAYERS, 2)),
            dma((2, 4, LAYERS, 2)),
            dma((2, 2, 2, 2)),
            dma((2,)),
            dma((2, NY)),
            dma((LAYERS, 4, 2)),
            dma((LAYERS,)),
            dma((2, 4, LAYERS, 2)),
            dma((2, 4, LAYERS, 2)),
            dma((2, LAYERS)),
            dma((2, 2, 2)),
            dma((LAYERS,)),
        ],
        compiler_params=pltpu.CompilerParams(
            collective_id=0, has_side_effects=True, vmem_limit_bytes=48 * 1024 * 1024
        ),
    )(*args)
    return pl.pallas_call(
        place_kernel,
        out_shape=(jax.ShapeDtypeStruct(actor_weights.shape, BF16), state, state, state),
        in_specs=[anywhere] * 4,
        out_specs=[anywhere] * 4,
        scratch_shapes=[dma((NY + 3,))],
        compiler_params=pltpu.CompilerParams(vmem_limit_bytes=4 * 1024 * 1024),
    )(*results)


def solution(mesh):
    in_specs = (
        P("rep", None, "grp", None),
        P(None, "grp", "rep"),
        P(None, "grp", "rep"),
        P(None, "grp", "rep"),
        P(None, "grp", None),
    )
    out_specs = (
        P(None, "grp", None),
        P(None, "grp", "rep"),
        P(None, "grp", "rep"),
        P(None, "grp", "rep"),
    )
    return jax.shard_map(body, mesh=mesh, in_specs=in_specs, out_specs=out_specs, check_vma=False)
```

```python
import jax
import jax.numpy as jnp
from jax import lax
from jax.experimental import pallas as pl
from jax.experimental.pallas import tpu as pltpu
from jax.sharding import PartitionSpec as P

MESH = pl.DeviceIdType.MESH

bias_one = 0.9999734386011124
bias_two = 0.09520785288629106
learn_rate = 0.01
decay_rate = 0.1

NY = 8
LAYERS = 2
ROWS = 160
HALF = ROWS // 2
COLS = 128
PIECE = 16
SPAN = 640
Z_ORDER = (0, 4, 2, 6, 1, 5, 3, 7)
F32 = jnp.float32
BF16 = jnp.bfloat16


def kernel(
    grad, master, first, second, actor,
    new_actor, new_master, new_first, new_second,
    grad_v, master_v, first_v, second_v, actor_v,
    sum_recv, sum_send, last_recv, raw_recv, one_recv, one_send, swapped, total,
    padded, delta_send, delta_recv, piece,
    load_sem, store_sem, rs_send, rs_recv, last_sems, raw_sems, swap_sems, move_send, move_recv, ag_send, ag_recv, ag_cross, ag_over, piece_sem,
):
    r, g = lax.axis_index("rep"), lax.axis_index("grp")
    y, h = r // 2, r % 2
    z, lo, core = g // 4, (g // 2) % 2, g % 2
    ring = (((y + 1) % NY) * 2 + h, ((y + NY - 1) % NY) * 2 + h)
    beyond = (((y + 2) % NY) * 2 + h, ((y + NY - 2) % NY) * 2 + h)
    across = (((y + 1) % NY) * 2 + 1 - h, ((y + NY - 1) % NY) * 2 + 1 - h)
    far = (((y + 2) % NY) * 2 + 1 - h, ((y + NY - 2) % NY) * 2 + 1 - h)
    partner = y * 2 + (1 - h)

    def at(dy):
        return (y + dy + 2 * NY) % NY

    def flip(bit, by):
        return (bit + by) % 2

    def remote(source, target, send_sem, recv_sem, rep, grp):
        return pltpu.make_async_remote_copy(
            src_ref=source, dst_ref=target, send_sem=send_sem, recv_sem=recv_sem,
            device_id={"rep": rep, "grp": grp}, device_id_type=MESH,
        )

    grad_load = pltpu.make_async_copy(grad.at[0], grad_v, load_sem.at[0])
    grad_load.start()
    unit = pl.ds(pl.multiple_of((y // 2) * PIECE, PIECE), PIECE)
    first_z = 2 * flip(h, core) + 1 - y % 2
    loads = [
        pltpu.make_async_copy(master, master_v, load_sem.at[1]),
        pltpu.make_async_copy(first, first_v, load_sem.at[2]),
        pltpu.make_async_copy(second, second_v, load_sem.at[3]),
    ]
    for t in range(2):
        rows = pl.ds(pl.multiple_of((first_z + 4 * t) * SPAN, 128), SPAN)
        loads.append(pltpu.make_async_copy(actor.at[:, unit, rows], actor_v.at[t], load_sem.at[4 + t]))
    for load in loads:
        load.start()

    def target(to, other):
        return (2 * to + 1 - z % 2) * 2 + flip((z // 2) % 2, other), 2 * r + other

    barrier = pltpu.get_barrier_semaphore()
    greeted = [(peer, g) for peer in (*ring, *beyond, *across, *far, partner)]
    greeted += [target(to, other) for to in range(4) for other in range(2)]
    greeted += [(2 * z + lo, 4 * (first_z + 4 * t) + j) for t in range(2) for j in range(4)]
    for rep, grp in greeted:
        pl.semaphore_signal(barrier, inc=1, device_id={"rep": rep, "grp": grp}, device_id_type=MESH)
    padded[...] = jnp.zeros_like(padded)
    pl.semaphore_wait(barrier, len(greeted))

    def dest_of(way, hops):
        return at(hops if way == 0 else -hops)

    def both(dest):
        return pl.ds(pl.multiple_of(dest * 2 * COLS, 2 * COLS), 2 * COLS)

    def one(dest, owner):
        return pl.ds(pl.multiple_of((dest * 2 + owner) * COLS, COLS), COLS)

    def rs_copy(way, hops, layer, half, own=False):
        rows = pl.ds(half * HALF, HALF)
        if layer == 1:
            source, place = one_send.at[way, hops - 1, rows], one_recv.at[way, hops - 1, rows]
        else:
            place = sum_recv.at[way, hops - 1, rows]
            source = grad_v.at[0, rows, both(dest_of(way, hops))] if own else sum_send.at[way, hops - 1, rows]
        return remote(
            source, place, rs_send.at[way, hops - 1, layer, half], rs_recv.at[way, hops - 1, layer, half],
            beyond[way] if hops == 4 else ring[way], g,
        )

    def last_copy(way, half, other):
        rows, owner = rows_of(half), 1 - h if other else h
        return remote(
            sum_send.at[way, 0, rows, pl.ds(pl.multiple_of(owner * COLS, COLS), COLS)],
            last_recv.at[way, other, rows], last_sems.at[0, way, half, other], last_sems.at[1, way, half, other],
            across[way] if other else ring[way], g,
        )

    def raw_copy():
        return remote(
            grad_v.at[0, :, one(y, 1 - h)], raw_recv, raw_sems.at[0], raw_sems.at[1], partner, g
        )

    def swap(offset):
        return remote(
            grad_v.at[1, :, one(at(offset), 1 - h)], swapped.at[offset % NY],
            swap_sems.at[0, offset % NY], swap_sems.at[1, offset % NY], partner, g,
        )

    sent = []

    def start(copy):
        copy.start()
        sent.append(copy)

    def rows_of(half):
        return pl.ds(half * HALF, HALF)

    def with_swapped(offset, rows):
        return grad_v[1, rows, one(at(offset), h)].astype(F32) + swapped[offset % NY, rows, :].astype(F32)

    grad_load.wait()
    for offset in (4, 3, -3):
        start(swap(offset))
    for half in range(2):
        start(rs_copy(half, 4, 0, half, True))
        for way in range(2):
            start(rs_copy(way, 3, 0, half, True))
    for offset in (2, -2, 1, -1, 0):
        start(swap(offset))
    start(raw_copy())
    swap(4).wait_recv()
    for way in range(2):
        one_send[way, 3, rows_of(way), :] = with_swapped(4, rows_of(way)).astype(BF16)
        start(rs_copy(way, 4, 1, way))
    for way in range(2):
        swap(3 if way == 0 else -3).wait_recv()
        for half in range(2):
            one_send[way, 2, rows_of(half), :] = with_swapped(3 if way == 0 else -3, rows_of(half)).astype(BF16)
            start(rs_copy(way, 3, 1, half))
    for hops in (2, 1):
        for half in range(2):
            for way in range(2):
                rows = rows_of(half)
                rs_copy(way, hops + 1, 0, half, True).wait_recv()
                summed = grad_v[0, rows, both(dest_of(way, hops))].astype(F32)
                summed = summed + sum_recv[way, hops, rows, :].astype(F32)
                if hops == 2 and half == way:
                    rs_copy(way, 4, 0, half, True).wait_recv()
                    summed = summed + sum_recv[way, 3, rows, :].astype(F32)
                sum_send[way, hops - 1, rows, :] = summed.astype(BF16)
                if hops == 2:
                    start(rs_copy(way, 2, 0, half))
                else:
                    for other in (1, 0):
                        start(last_copy(way, half, other))
        for way in range(2):
            swap(hops if way == 0 else -hops).wait_recv()
        for half in range(2):
            for way in range(2):
                rows = rows_of(half)
                rs_copy(way, hops + 1, 1, half).wait_recv()
                summed = with_swapped(hops if way == 0 else -hops, rows) + one_recv[way, hops, rows, :].astype(F32)
                if hops == 2 and half == way:
                    rs_copy(way, 4, 1, half).wait_recv()
                    summed = summed + one_recv[way, 3, rows, :].astype(F32)
                one_send[way, hops - 1, rows, :] = summed.astype(BF16)
                start(rs_copy(way, hops, 1, half))

    raw_copy().wait_recv()
    for half in range(2):
        rows = rows_of(half)
        summed = grad_v[0, rows, one(y, h)].astype(F32) + raw_recv[rows, :].astype(F32)
        for way in range(2):
            for other in range(2):
                last_copy(way, half, other).wait_recv()
                summed = summed + last_recv[way, other, rows, :].astype(F32)
        total[0, rows, :] = summed

    def finish_one():
        swap(0).wait_recv()
        for half in range(2):
            for way in range(2):
                rs_copy(way, 1, 1, half).wait_recv()
            rows = rows_of(half)
            summed = with_swapped(0, rows)
            for way in range(2):
                summed = summed + one_recv[way, 0, rows, :].astype(F32)
            total[1, rows, :] = summed

    for load in loads:
        load.wait()
    slot = (z // 4) * 4 + g % 4
    shift = pl.multiple_of((g % 4) * 32, 32)
    stores = []
    for layer in range(LAYERS):
        if layer == 1:
            finish_one()
        gradient = total[layer]
        moment = 0.9 * first_v[layer] + 0.1 * gradient
        square = 0.999 * second_v[layer] + 0.001 * gradient * gradient
        weight = master_v[layer]
        update = moment * (1.0 / bias_one) / (jnp.sqrt(square * (1.0 / bias_two)) + 1e-08) + decay_rate * weight
        step = -learn_rate * update
        padded[layer, pl.ds(shift, ROWS), :] = step
        delta_send[layer] = padded[layer].T.astype(BF16)
        for to in range(4):
            for other in range(2):
                start(
                    remote(
                        delta_send.at[layer, pl.ds(other * 64 + to * PIECE, PIECE)], delta_recv.at[layer, slot],
                        move_send.at[layer, to, other], move_recv.at[layer], *target(to, other),
                    )
                )
        master_v[layer] = weight + step
        first_v[layer] = moment
        second_v[layer] = square
        for index, (array, result) in enumerate(
            ((master_v, new_master), (first_v, new_first), (second_v, new_second))
        ):
            store = pltpu.make_async_copy(array.at[layer], result.at[layer], store_sem.at[index, layer])
            store.start()
            stores.append(store)

    def region(origin, owner, layer, half=None):
        z_block = (1 - origin % 2) * 4 + flip(owner, core) * 2
        z_range = pl.ds(z_block, 2) if half is None else pl.ds(z_block + half, 1)
        return new_actor.at[layer, z_range, pl.ds(pl.multiple_of((origin // 2) * PIECE, PIECE), PIECE)]

    def ag_copy(way, hops, layer, other):
        held = 2 if hops == 4 else hops - 1
        goes_across = other and hops in ((1,), (3, 4))[layer]
        owner = 1 - h if other and not goes_across else h
        place = region(at(-held if way == 0 else held), owner, layer, way if hops == 4 else None)
        near = across if goes_across else ring
        return remote(
            piece.at[layer] if hops == 1 else place, place,
            ag_send.at[way, hops - 1, layer, other], ag_recv.at[way, hops - 1, layer, other],
            (far if goes_across else beyond)[way] if hops == 4 else near[way], g,
        )

    def ag_cross_copy(layer):
        return remote(
            piece.at[layer], region(y, h, layer), ag_cross.at[0, layer], ag_cross.at[1, layer], partner, g
        )

    for layer in range(LAYERS):
        pltpu.make_async_copy(delta_recv.at[layer], delta_recv.at[layer], move_recv.at[layer]).wait()
        for t in range(2):
            low = [delta_recv[layer, 4 * t + j, :, :128].astype(F32) for j in range(4)]
            high = [delta_recv[layer, 4 * t + j, :, 128:].astype(F32) for j in range(4)]
            tiles = [low[0], high[0] + low[1], high[1] + low[2], high[2] + low[3], high[3]]
            for index, tile in enumerate(tiles):
                place = slice(index * 128, index * 128 + 128)
                piece[layer, t, :, place] = (actor_v[t, layer, :, place].astype(F32) + tile).astype(BF16)
        for way in range(2):
            start(ag_copy(way, 1, layer, 0))
            if layer == 0:
                start(ag_copy(way, 1, 0, 1))
        start(ag_cross_copy(layer))
        store = pltpu.make_async_copy(piece.at[layer], region(y, h, layer), piece_sem.at[layer])
        store.start()
        stores.append(store)

    def both_copy(way, hops):
        held = 2 if hops == 4 else hops - 1
        origin = at(-held if way == 0 else held)
        z_block = (1 - origin % 2) * 4
        z_range = pl.ds(z_block + 2 * way, 2) if hops == 4 else pl.ds(z_block, 4)
        place = new_actor.at[0, z_range, pl.ds(pl.multiple_of((origin // 2) * PIECE, PIECE), PIECE)]
        return remote(
            place, place, ag_send.at[way, hops - 1, 0, 0], ag_recv.at[way, hops - 1, 0, 0],
            (beyond if hops == 4 else ring)[way], g,
        )

    def gather_both(come):
        for way in range(2):
            if come == 1:
                for other in range(2):
                    ag_copy(way, 1, 0, other).wait_recv()
            else:
                both_copy(way, come).wait_recv()
            for to in (4, 3) if come == 2 else (2,):
                start(both_copy(way, to))

    def over(hops, way, other):
        place = region(at(-hops if way == 0 else hops), 1 - h if other else h, 1)
        return remote(place, place, ag_over.at[0, way, hops - 1], ag_over.at[1, way, hops - 1], partner, g)

    def gather_one(come):
        for way in range(2):
            ag_copy(way, come, 1, 0).wait_recv()
            for to in (4, 3) if come == 2 else (2,):
                start(ag_copy(way, to, 1, 0))
                if come == 2:
                    start(ag_copy(way, to, 1, 1))
            start(over(come, way, 0))

    gather_both(1)
    gather_one(1)
    gather_both(2)
    gather_one(2)
    for layer in range(LAYERS):
        ag_cross_copy(layer).wait_recv()
    for way in range(2):
        for hops in (1, 2):
            over(hops, way, 1).wait_recv()
        for hops in (3, 4):
            both_copy(way, hops).wait_recv()
            for other in range(2):
                ag_copy(way, hops, 1, other).wait_recv()

    for copy in sent:
        copy.wait_send()
    for store in stores:
        store.wait()


def place_kernel(actor, master, first, second, new_actor, new_master, new_first, new_second, sems):
    copies = [
        pltpu.make_async_copy(
            actor.at[:, index], new_actor.at[:, :, pl.ds(place * SPAN, SPAN)], sems.at[index]
        )
        for index, place in enumerate(Z_ORDER)
    ]
    for index, (array, result) in enumerate(((master, new_master), (first, new_first), (second, new_second))):
        copies.append(pltpu.make_async_copy(array, result, sems.at[NY + index]))
    for copy in copies:
        copy.start()
    for copy in copies:
        copy.wait()


def body(grad_parts, master, first_moment, second_moment, actor_weights):
    args = [
        pltpu.with_memory_space_constraint(array, pltpu.HBM)
        for array in (grad_parts, master, first_moment, second_moment, actor_weights)
    ]
    anywhere = pl.BlockSpec(memory_space=pl.ANY)
    state = jax.ShapeDtypeStruct(master.shape, F32)
    state_v = pltpu.VMEM((LAYERS, ROWS, COLS), F32)
    dma = pltpu.SemaphoreType.DMA
    results = pl.pallas_call(
        kernel,
        out_shape=(jax.ShapeDtypeStruct((LAYERS, NY, 64, SPAN), BF16), state, state, state),
        in_specs=[anywhere] * 5,
        out_specs=[anywhere] * 4,
        scratch_shapes=[
            pltpu.VMEM((LAYERS, ROWS, 2048), BF16),
            state_v,
            state_v,
            state_v,
            pltpu.VMEM((2, LAYERS, PIECE, SPAN), BF16),
            pltpu.VMEM((2, 4, ROWS, 2 * COLS), BF16),
            pltpu.VMEM((2, 2, ROWS, 2 * COLS), BF16),
            pltpu.VMEM((2, 2, ROWS, COLS), BF16),
            pltpu.VMEM((ROWS, COLS), BF16),
            pltpu.VMEM((2, 4, ROWS, COLS), BF16),
            pltpu.VMEM((2, 4, ROWS, COLS), BF16),
            pltpu.VMEM((NY, ROWS, COLS), BF16),
            state_v,
            pltpu.VMEM((LAYERS, 256, COLS), F32),
            pltpu.VMEM((LAYERS, COLS, 256), BF16),
            pltpu.VMEM((LAYERS, 8, PIECE, 256), BF16),
            pltpu.VMEM((LAYERS, 2, PIECE, SPAN), BF16),
            dma((6,)),
            dma((3, LAYERS)),
            dma((2, 4, LAYERS, 2)),
            dma((2, 4, LAYERS, 2)),
            dma((2, 2, 2, 2)),
            dma((2,)),
            dma((2, NY)),
            dma((LAYERS, 4, 2)),
            dma((LAYERS,)),
            dma((2, 4, LAYERS, 2)),
            dma((2, 4, LAYERS, 2)),
            dma((2, LAYERS)),
            dma((2, 2, 2)),
            dma((LAYERS,)),
        ],
        compiler_params=pltpu.CompilerParams(
            collective_id=0, has_side_effects=True, vmem_limit_bytes=48 * 1024 * 1024
        ),
    )(*args)
    return pl.pallas_call(
        place_kernel,
        out_shape=(jax.ShapeDtypeStruct(actor_weights.shape, BF16), state, state, state),
        in_specs=[anywhere] * 4,
        out_specs=[anywhere] * 4,
        scratch_shapes=[dma((NY + 3,))],
        compiler_params=pltpu.CompilerParams(vmem_limit_bytes=4 * 1024 * 1024),
    )(*results)


def solution(mesh):
    in_specs = (
        P("rep", None, "grp", None),
        P(None, "grp", "rep"),
        P(None, "grp", "rep"),
        P(None, "grp", "rep"),
        P(None, "grp", None),
    )
    out_specs = (
        P(None, "grp", None),
        P(None, "grp", "rep"),
        P(None, "grp", "rep"),
        P(None, "grp", "rep"),
    )
    return jax.shard_map(body, mesh=mesh, in_specs=in_specs, out_specs=out_specs, check_vma=False)
```

```python
import jax
import jax.numpy as jnp
from jax import lax
from jax.experimental import pallas as pl
from jax.experimental.pallas import tpu as pltpu
from jax.sharding import PartitionSpec as P

MESH = pl.DeviceIdType.MESH

bias_one = 0.9999734386011124
bias_two = 0.09520785288629106
learn_rate = 0.01
decay_rate = 0.1

NY = 8
LAYERS = 2
ROWS = 160
HALF = ROWS // 2
COLS = 128
PIECE = 16
SPAN = 640
Z_ORDER = (0, 4, 2, 6, 1, 5, 3, 7)
F32 = jnp.float32
BF16 = jnp.bfloat16


def kernel(
    grad, master, first, second, actor,
    new_actor, new_master, new_first, new_second,
    grad_v, master_v, first_v, second_v, actor_v,
    sum_recv, sum_send, last_recv, raw_recv, one_recv, one_send, swapped, total,
    padded, delta_send, delta_recv, piece,
    load_sem, store_sem, rs_send, rs_recv, last_sems, raw_sems, swap_sems, move_send, move_recv, ag_send, ag_recv, ag_cross, ag_over, piece_sem,
):
    r, g = lax.axis_index("rep"), lax.axis_index("grp")
    y, h = r // 2, r % 2
    z, lo, core = g // 4, (g // 2) % 2, g % 2
    ring = (((y + 1) % NY) * 2 + h, ((y + NY - 1) % NY) * 2 + h)
    beyond = (((y + 2) % NY) * 2 + h, ((y + NY - 2) % NY) * 2 + h)
    across = (((y + 1) % NY) * 2 + 1 - h, ((y + NY - 1) % NY) * 2 + 1 - h)
    far = (((y + 2) % NY) * 2 + 1 - h, ((y + NY - 2) % NY) * 2 + 1 - h)
    partner = y * 2 + (1 - h)

    def at(dy):
        return (y + dy + 2 * NY) % NY

    def flip(bit, by):
        return (bit + by) % 2

    def remote(source, target, send_sem, recv_sem, rep, grp):
        return pltpu.make_async_remote_copy(
            src_ref=source, dst_ref=target, send_sem=send_sem, recv_sem=recv_sem,
            device_id={"rep": rep, "grp": grp}, device_id_type=MESH,
        )

    grad_load = pltpu.make_async_copy(grad.at[0], grad_v, load_sem.at[0])
    grad_load.start()
    unit = pl.ds(pl.multiple_of((y // 2) * PIECE, PIECE), PIECE)
    first_z = 2 * flip(h, core) + 1 - y % 2
    loads = [
        pltpu.make_async_copy(master, master_v, load_sem.at[1]),
        pltpu.make_async_copy(first, first_v, load_sem.at[2]),
        pltpu.make_async_copy(second, second_v, load_sem.at[3]),
    ]
    for t in range(2):
        rows = pl.ds(pl.multiple_of((first_z + 4 * t) * SPAN, 128), SPAN)
        loads.append(pltpu.make_async_copy(actor.at[:, unit, rows], actor_v.at[t], load_sem.at[4 + t]))
    for load in loads:
        load.start()

    def target(to, other):
        return (2 * to + 1 - z % 2) * 2 + flip((z // 2) % 2, other), 2 * r + other

    barrier = pltpu.get_barrier_semaphore()
    greeted = [(peer, g) for peer in (*ring, *beyond, *across, *far, partner)]
    greeted += [target(to, other) for to in range(4) for other in range(2)]
    greeted += [(2 * z + lo, 4 * (first_z + 4 * t) + j) for t in range(2) for j in range(4)]
    for rep, grp in greeted:
        pl.semaphore_signal(barrier, inc=1, device_id={"rep": rep, "grp": grp}, device_id_type=MESH)
    padded[...] = jnp.zeros_like(padded)
    pl.semaphore_wait(barrier, len(greeted))

    def dest_of(way, hops):
        return at(hops if way == 0 else -hops)

    def both(dest):
        return pl.ds(pl.multiple_of(dest * 2 * COLS, 2 * COLS), 2 * COLS)

    def one(dest, owner):
        return pl.ds(pl.multiple_of((dest * 2 + owner) * COLS, COLS), COLS)

    def rs_copy(way, hops, layer, half, own=False):
        rows = pl.ds(half * HALF, HALF)
        if layer == 1:
            source, place = one_send.at[way, hops - 1, rows], one_recv.at[way, hops - 1, rows]
        else:
            place = sum_recv.at[way, hops - 1, rows]
            source = grad_v.at[0, rows, both(dest_of(way, hops))] if own else sum_send.at[way, hops - 1, rows]
        return remote(
            source, place, rs_send.at[way, hops - 1, layer, half], rs_recv.at[way, hops - 1, layer, half],
            beyond[way] if hops == 4 else ring[way], g,
        )

    def last_copy(way, half, other):
        rows, owner = rows_of(half), 1 - h if other else h
        return remote(
            sum_send.at[way, 0, rows, pl.ds(pl.multiple_of(owner * COLS, COLS), COLS)],
            last_recv.at[way, other, rows], last_sems.at[0, way, half, other], last_sems.at[1, way, half, other],
            across[way] if other else ring[way], g,
        )

    def raw_copy():
        return remote(
            grad_v.at[0, :, one(y, 1 - h)], raw_recv, raw_sems.at[0], raw_sems.at[1], partner, g
        )

    def swap(offset):
        return remote(
            grad_v.at[1, :, one(at(offset), 1 - h)], swapped.at[offset % NY],
            swap_sems.at[0, offset % NY], swap_sems.at[1, offset % NY], partner, g,
        )

    sent = []

    def start(copy):
        copy.start()
        sent.append(copy)

    def rows_of(half):
        return pl.ds(half * HALF, HALF)

    def with_swapped(offset, rows):
        return grad_v[1, rows, one(at(offset), h)].astype(F32) + swapped[offset % NY, rows, :].astype(F32)

    grad_load.wait()
    start(swap(4))
    for half in range(2):
        start(rs_copy(half, 4, 0, half, True))
        for way in range(2):
            start(rs_copy(way, 3, 0, half, True))
    for offset in (3, -3, 2, -2, 1, -1, 0):
        start(swap(offset))
    start(raw_copy())
    swap(4).wait_recv()
    for way in range(2):
        one_send[way, 3, rows_of(way), :] = with_swapped(4, rows_of(way)).astype(BF16)
        start(rs_copy(way, 4, 1, way))
    for way in range(2):
        swap(3 if way == 0 else -3).wait_recv()
        for half in range(2):
            one_send[way, 2, rows_of(half), :] = with_swapped(3 if way == 0 else -3, rows_of(half)).astype(BF16)
            start(rs_copy(way, 3, 1, half))
    for hops in (2, 1):
        for half in range(2):
            for way in range(2):
                rows = rows_of(half)
                rs_copy(way, hops + 1, 0, half, True).wait_recv()
                summed = grad_v[0, rows, both(dest_of(way, hops))].astype(F32)
                summed = summed + sum_recv[way, hops, rows, :].astype(F32)
                if hops == 2 and half == way:
                    rs_copy(way, 4, 0, half, True).wait_recv()
                    summed = summed + sum_recv[way, 3, rows, :].astype(F32)
                sum_send[way, hops - 1, rows, :] = summed.astype(BF16)
                if hops == 2:
                    start(rs_copy(way, 2, 0, half))
                else:
                    for other in (1, 0):
                        start(last_copy(way, half, other))
        for way in range(2):
            swap(hops if way == 0 else -hops).wait_recv()
        for half in range(2):
            for way in range(2):
                rows = rows_of(half)
                rs_copy(way, hops + 1, 1, half).wait_recv()
                summed = with_swapped(hops if way == 0 else -hops, rows) + one_recv[way, hops, rows, :].astype(F32)
                if hops == 2 and half == way:
                    rs_copy(way, 4, 1, half).wait_recv()
                    summed = summed + one_recv[way, 3, rows, :].astype(F32)
                one_send[way, hops - 1, rows, :] = summed.astype(BF16)
                start(rs_copy(way, hops, 1, half))

    raw_copy().wait_recv()
    for half in range(2):
        rows = rows_of(half)
        summed = grad_v[0, rows, one(y, h)].astype(F32) + raw_recv[rows, :].astype(F32)
        for way in range(2):
            for other in range(2):
                last_copy(way, half, other).wait_recv()
                summed = summed + last_recv[way, other, rows, :].astype(F32)
        total[0, rows, :] = summed

    def finish_one():
        swap(0).wait_recv()
        for half in range(2):
            for way in range(2):
                rs_copy(way, 1, 1, half).wait_recv()
            rows = rows_of(half)
            summed = with_swapped(0, rows)
            for way in range(2):
                summed = summed + one_recv[way, 0, rows, :].astype(F32)
            total[1, rows, :] = summed

    for load in loads:
        load.wait()
    slot = (z // 4) * 4 + g % 4
    shift = pl.multiple_of((g % 4) * 32, 32)
    stores = []
    for layer in range(LAYERS):
        if layer == 1:
            finish_one()
        gradient = total[layer]
        moment = 0.9 * first_v[layer] + 0.1 * gradient
        square = 0.999 * second_v[layer] + 0.001 * gradient * gradient
        weight = master_v[layer]
        update = moment * (1.0 / bias_one) / (jnp.sqrt(square * (1.0 / bias_two)) + 1e-08) + decay_rate * weight
        step = -learn_rate * update
        padded[layer, pl.ds(shift, ROWS), :] = step
        delta_send[layer] = padded[layer].T.astype(BF16)
        for to in range(4):
            for other in range(2):
                start(
                    remote(
                        delta_send.at[layer, pl.ds(other * 64 + to * PIECE, PIECE)], delta_recv.at[layer, slot],
                        move_send.at[layer, to, other], move_recv.at[layer], *target(to, other),
                    )
                )
        master_v[layer] = weight + step
        first_v[layer] = moment
        second_v[layer] = square
        for index, (array, result) in enumerate(
            ((master_v, new_master), (first_v, new_first), (second_v, new_second))
        ):
            store = pltpu.make_async_copy(array.at[layer], result.at[layer], store_sem.at[index, layer])
            store.start()
            stores.append(store)

    def region(origin, owner, layer, half=None):
        z_block = (1 - origin % 2) * 4 + flip(owner, core) * 2
        z_range = pl.ds(z_block, 2) if half is None else pl.ds(z_block + half, 1)
        return new_actor.at[layer, z_range, pl.ds(pl.multiple_of((origin // 2) * PIECE, PIECE), PIECE)]

    def ag_copy(way, hops, layer, other, t):
        held = 2 if hops == 4 else hops - 1
        goes_across = other and hops in ((1,), (3, 4))[layer]
        owner = 1 - h if other and not goes_across else h
        place = region(at(-held if way == 0 else held), owner, layer, t)
        near = across if goes_across else ring
        return remote(
            piece.at[layer, pl.ds(t, 1)] if hops == 1 else place, place,
            ag_send.at[way, hops - 1, layer, other, t], ag_recv.at[way, hops - 1, layer, other, t],
            (far if goes_across else beyond)[way] if hops == 4 else near[way], g,
        )

    def ag_cross_copy(layer):
        return remote(
            piece.at[layer], region(y, h, layer), ag_cross.at[0, layer], ag_cross.at[1, layer], partner, g
        )

    for layer in range(LAYERS):
        pltpu.make_async_copy(delta_recv.at[layer], delta_recv.at[layer], move_recv.at[layer]).wait()
        for t in range(2):
            low = [delta_recv[layer, 4 * t + j, :, :128].astype(F32) for j in range(4)]
            high = [delta_recv[layer, 4 * t + j, :, 128:].astype(F32) for j in range(4)]
            tiles = [low[0], high[0] + low[1], high[1] + low[2], high[2] + low[3], high[3]]
            for index, tile in enumerate(tiles):
                place = slice(index * 128, index * 128 + 128)
                piece[layer, t, :, place] = (actor_v[t, layer, :, place].astype(F32) + tile).astype(BF16)
            for way in range(2):
                start(ag_copy(way, 1, layer, 0, t))
                if layer == 0:
                    start(ag_copy(way, 1, 0, 1, t))
        start(ag_cross_copy(layer))
        store = pltpu.make_async_copy(piece.at[layer], region(y, h, layer), piece_sem.at[layer])
        store.start()
        stores.append(store)

    def over(hops, way, other):
        place = region(at(-hops if way == 0 else hops), 1 - h if other else h, 1)
        return remote(place, place, ag_over.at[0, way, hops - 1], ag_over.at[1, way, hops - 1], partner, g)

    def gather(come, layer, other):
        for t in range(2):
            for way in range(2):
                ag_copy(way, come, layer, other, t).wait_recv()
                for to in (4, 3) if come == 2 else (2,):
                    if to < 4 or t == way:
                        start(ag_copy(way, to, layer, other, t))
                        if layer == 1 and come == 2:
                            start(ag_copy(way, to, 1, 1, t))
        if layer == 1:
            for way in range(2):
                start(over(come, way, 0))

    gather(1, 0, 0)
    gather(1, 1, 0)
    gather(1, 0, 1)
    gather(2, 1, 0)
    gather(2, 0, 0)
    gather(2, 0, 1)
    for layer in range(LAYERS):
        ag_cross_copy(layer).wait_recv()
    for way in range(2):
        for hops in (1, 2):
            over(hops, way, 1).wait_recv()
        for hops in (3, 4):
            for layer in range(LAYERS):
                for other in range(2):
                    for t in range(2) if hops == 3 else (way,):
                        ag_copy(way, hops, layer, other, t).wait_recv()

    for copy in sent:
        copy.wait_send()
    for store in stores:
        store.wait()


def place_kernel(actor, master, first, second, new_actor, new_master, new_first, new_second, sems):
    copies = [
        pltpu.make_async_copy(
            actor.at[:, index], new_actor.at[:, :, pl.ds(place * SPAN, SPAN)], sems.at[index]
        )
        for index, place in enumerate(Z_ORDER)
    ]
    for index, (array, result) in enumerate(((master, new_master), (first, new_first), (second, new_second))):
        copies.append(pltpu.make_async_copy(array, result, sems.at[NY + index]))
    for copy in copies:
        copy.start()
    for copy in copies:
        copy.wait()


def body(grad_parts, master, first_moment, second_moment, actor_weights):
    args = [
        pltpu.with_memory_space_constraint(array, pltpu.HBM)
        for array in (grad_parts, master, first_moment, second_moment, actor_weights)
    ]
    anywhere = pl.BlockSpec(memory_space=pl.ANY)
    state = jax.ShapeDtypeStruct(master.shape, F32)
    state_v = pltpu.VMEM((LAYERS, ROWS, COLS), F32)
    dma = pltpu.SemaphoreType.DMA
    results = pl.pallas_call(
        kernel,
        out_shape=(jax.ShapeDtypeStruct((LAYERS, NY, 64, SPAN), BF16), state, state, state),
        in_specs=[anywhere] * 5,
        out_specs=[anywhere] * 4,
        scratch_shapes=[
            pltpu.VMEM((LAYERS, ROWS, 2048), BF16),
            state_v,
            state_v,
            state_v,
            pltpu.VMEM((2, LAYERS, PIECE, SPAN), BF16),
            pltpu.VMEM((2, 4, ROWS, 2 * COLS), BF16),
            pltpu.VMEM((2, 2, ROWS, 2 * COLS), BF16),
            pltpu.VMEM((2, 2, ROWS, COLS), BF16),
            pltpu.VMEM((ROWS, COLS), BF16),
            pltpu.VMEM((2, 4, ROWS, COLS), BF16),
            pltpu.VMEM((2, 4, ROWS, COLS), BF16),
            pltpu.VMEM((NY, ROWS, COLS), BF16),
            state_v,
            pltpu.VMEM((LAYERS, 256, COLS), F32),
            pltpu.VMEM((LAYERS, COLS, 256), BF16),
            pltpu.VMEM((LAYERS, 8, PIECE, 256), BF16),
            pltpu.VMEM((LAYERS, 2, PIECE, SPAN), BF16),
            dma((6,)),
            dma((3, LAYERS)),
            dma((2, 4, LAYERS, 2)),
            dma((2, 4, LAYERS, 2)),
            dma((2, 2, 2, 2)),
            dma((2,)),
            dma((2, NY)),
            dma((LAYERS, 4, 2)),
            dma((LAYERS,)),
            dma((2, 4, LAYERS, 2, 2)),
            dma((2, 4, LAYERS, 2, 2)),
            dma((2, LAYERS)),
            dma((2, 2, 2)),
            dma((LAYERS,)),
        ],
        compiler_params=pltpu.CompilerParams(
            collective_id=0, has_side_effects=True, vmem_limit_bytes=48 * 1024 * 1024
        ),
    )(*args)
    return pl.pallas_call(
        place_kernel,
        out_shape=(jax.ShapeDtypeStruct(actor_weights.shape, BF16), state, state, state),
        in_specs=[anywhere] * 4,
        out_specs=[anywhere] * 4,
        scratch_shapes=[dma((NY + 3,))],
        compiler_params=pltpu.CompilerParams(vmem_limit_bytes=4 * 1024 * 1024),
    )(*results)


def solution(mesh):
    in_specs = (
        P("rep", None, "grp", None),
        P(None, "grp", "rep"),
        P(None, "grp", "rep"),
        P(None, "grp", "rep"),
        P(None, "grp", None),
    )
    out_specs = (
        P(None, "grp", None),
        P(None, "grp", "rep"),
        P(None, "grp", "rep"),
        P(None, "grp", "rep"),
    )
    return jax.shard_map(body, mesh=mesh, in_specs=in_specs, out_specs=out_specs, check_vma=False)
```
